1024 devices in a mesh: domain: 64 (over x, z_lo, core), panel: 16 (over z_hi, y).
Axes of the slice: x: 4, y: 4, z: 32 (z_hi: 4, z_lo: 8; z = z_hi * 8 + z_lo), core: 2. Of those that a mesh axis runs over, the one named last changes fastest.
Arguments:
- eigvec: bfloat16 [98304, 8192], P('domain', 'panel'), may hold values from -0.01953125 to 0.01953125
- flux: bfloat16 [98304, 768], P('domain'), may hold values from -64 to 64
- blocks: int32 [256, 2], P('domain'), may hold values from 0 to 5, as said below
- tile_mask: int32 [16, 2, 4, 4], P('panel'), may hold values 0 or 1
- freq: bfloat16 [16, 512], P('panel'), may hold values from 0.5 to 2
Outputs:
- pair_self: float32 [16, 512, 512], P('panel', 'domain')
- pair_next: float32 [16, 512, 512], P('panel', 'domain')
- diffusivity: float32 [16, 512], P('panel', 'domain')
The draws below stay inside these ranges and needn't reach their ends.
Inputs may be any that keep to these rules, and one draw needn't show every extreme that they name: Atom block g, which is block g mod 4 of its slab of 4 blocks, lists two different blocks among itself and its two neighbours along the atom order, numbered in its slab extended by one block on each side (so entries lie in g mod 4 to g mod 4 + 2), the order being periodic. The first and the last block of every slab list the two blocks beside them.
All inputs are finite; a program needn't handle non-finite values. No bound on the sum of `tile_mask` on one device may be relied on, other than what follows from the above.
Results may differ from the reference program's by a relative error of at most 0.0029.
Values may be sent and summed in bfloat16 or wider, within the bound.
A program may use at most 32 MiB of HBM per device.

```python
import math
import jax
import jax.numpy as jnp
from jax import lax

BLK = 128
NB = 2
MODES = 512
TILE = 128
BLOCKS_DEV = 4
BLOCKS = 256
ROWS = 98304
PANELS = 16


def draw_blocks(key, part):
    key = jax.random.fold_in(key, 11)
    picks = jax.random.randint(key, (BLOCKS,), 0, 3)
    local = jnp.arange(BLOCKS, dtype=jnp.int32) % BLOCKS_DEV
    edge = (local == 0) | (local == BLOCKS_DEV - 1)
    picks = jnp.where(edge, 2, picks).astype(jnp.int32)
    first = local + jnp.where(picks == 1, 1, 0).astype(jnp.int32)
    second = local + jnp.where(picks == 0, 1, 2).astype(jnp.int32)
    return jnp.stack([first, second], axis=1).astype(jnp.int32)


def touch_ends(array, own_key, least, top_value):
    longest = array.shape.index(max(array.shape))
    spots = []
    for shift in (0, 1):
        where = [jax.random.randint(jax.random.fold_in(own_key, axis), (), 0, length) for axis, length in enumerate(array.shape)]
        where[longest] = (where[longest] + shift) % array.shape[longest]
        spots.append(tuple(where))
    return array.at[spots[0]].set(least).at[spots[1]].set(top_value)


def block_levels(own_key, shape, cuts, smallest, top_value):
    def one(dim, blocks):
        heights = jax.random.uniform(jax.random.fold_in(jax.random.fold_in(own_key, 6), dim), (blocks,), jnp.float32, smallest / len(cuts), top_value / len(cuts))
        return jnp.repeat(jnp.exp(heights), shape[dim] // blocks).reshape((-1,) + (1,) * (len(shape) - dim - 1))

    loudness = one(*cuts[0])
    for cut in cuts[1:]:
        loudness = loudness * one(*cut)
    return loudness


def normal_values(stream_key, dims, width, bound, cuts=(), kind=jnp.bfloat16):
    array = jax.random.normal(stream_key, dims, jnp.float32) * width
    if len(cuts) > 0:
        array = block_levels(stream_key, dims, cuts, -0.22, 0.18) * array
    return jnp.clip(array, min=-bound, max=bound).astype(kind)


def setup_inputs(seed: int = 0) -> dict:
    key_list = jax.random.split(jax.random.key(seed), 6)
    return {
        "eigvec": normal_values(key_list[0], (ROWS, PANELS * MODES), ROWS ** -0.5, 0.01953125, ((0, 64), (1, 16))),
        "flux": normal_values(key_list[1], (ROWS, NB * 3 * BLK), ((ROWS // (NB * 3 * BLK)) ** 0.5), 64.0, ((0, 64),)),
        "blocks": draw_blocks(jax.random.fold_in(key_list[5], 71), 0),
        "tile_mask": touch_ends((jax.random.randint(key_list[3], (PANELS, 2, MODES // TILE, MODES // TILE), 0, 4) < 3).astype(jnp.int32), jax.random.fold_in(key_list[3], 1), 0, 1),
        "freq": jnp.clip(0.5 + 1.5 * jax.random.uniform(key_list[4], (PANELS, MODES), jnp.float32) ** block_levels(key_list[4], (PANELS, MODES), ((0, 16),), -0.2, 0.2), 0.5, 2.0).astype(jnp.bfloat16),
    }


lorentz_width = 0.25


def lorentz(gap):
    return (lorentz_width / math.pi) / (gap * gap + lorentz_width * lorentz_width)


def reference(eigvec, flux, blocks, tile_mask, freq):
    span = 3 * BLK
    total_blocks = blocks.shape[0]
    index = jnp.arange(total_blocks, dtype=jnp.int32)
    first = index - index % BLOCKS_DEV
    source = ((first[:, None] + blocks - 1) % total_blocks).astype(jnp.int32)
    couplings = flux.reshape(total_blocks, span, NB * span).astype(jnp.float32)

    def image_of(panel):
        columns = lax.dynamic_slice_in_dim(eigvec, panel * MODES, MODES, 1).reshape(total_blocks, span, MODES)
        picked = jnp.take(columns, source, axis=0).reshape(total_blocks, NB * span, MODES).astype(jnp.float32)
        result = jnp.einsum("bij,bjm->bim", couplings, picked)
        return result.astype(jnp.bfloat16).reshape(total_blocks * span, MODES)

    panels = jnp.arange(PANELS, dtype=jnp.int32)
    images = lax.map(image_of, panels)

    def pairs_of(panel):
        columns = lax.dynamic_slice_in_dim(eigvec, panel * MODES, MODES, 1)
        following = images[jnp.minimum(panel + 1, PANELS - 1)] * (panel + 1 < PANELS).astype(jnp.bfloat16)
        own = jnp.dot(columns.T, images[panel], preferred_element_type=jnp.float32)
        ahead = jnp.dot(columns.T, following, preferred_element_type=jnp.float32)
        return own, ahead

    own, ahead = lax.map(pairs_of, panels)
    full = jnp.repeat(jnp.repeat(tile_mask, TILE, axis=2), TILE, axis=3).astype(jnp.float32)
    pair_self = own * full[:, 0]
    pair_next = ahead * full[:, 1]
    own_freq = freq.astype(jnp.float32)
    next_freq = jnp.concatenate([own_freq[1:], jnp.zeros((1, MODES), jnp.float32)], axis=0)
    weight_own = lorentz(own_freq[:, :, None] - own_freq[:, None, :])
    weight_next = lorentz(own_freq[:, :, None] - next_freq[:, None, :])
    total = jnp.sum(pair_self * pair_self * weight_own + pair_next * pair_next * weight_next, axis=2)
    diffusivity = (math.pi / 3.0) * total / (2.0 * MODES * own_freq * own_freq)
    return pair_self, pair_next, diffusivity
```

```python
import functools
import math

import jax
import jax.numpy as jnp
from jax import lax
from jax.experimental import pallas as pl
from jax.experimental.pallas import tpu as pltpu
from jax.sharding import PartitionSpec as P

MESH = pl.DeviceIdType.MESH
F32 = jnp.float32
BF16 = jnp.bfloat16

WIDTH = 0.25
SPAN = 384
MODES = 512
PART = 192
SELF, NEXT, PREV = 0, 1, 2
UP_ROWS = (0, 192, 1152, 1344)


def lorentz(gap):
    return WIDTH / math.pi / (gap * gap + WIDTH * WIDTH)


def mm(a, b):
    return jnp.dot(a, b, preferred_element_type=F32)


def mtm(a, b):
    return lax.dot_general(a, b, (((0,), (0,)), ((), ())), preferred_element_type=F32)


def kernel(
    e_ref, f_ref, blocks_ref, mask_ref, freq_ref,
    self_ref, next_ref, diff_ref,
    y_ref, halo, eprev, ynext, relay_up, relay_down,
    freq_mine, freq_next, pairs, core_in, x_out, x_in, z_out, z_in, prev_out, prev_in,
    halo_s, halo_r, up_s, up_r, down_s, down_r, relay_s, relay_r,
    freq_sem, core_sem, x_s, x_r, z_s, z_r, prev_sem,
):
    d = lax.axis_index("domain")
    p = lax.axis_index("panel")
    x, zl, c = d // 16, lax.rem(d // 2, 8), lax.rem(d, 2)
    y, zh = lax.rem(p, 4), p // 4
    has_next, has_prev = p < 15, p > 0
    rises, falls = zh < 3, zh > 0
    after, before = lax.rem(d + 1, 64), lax.rem(d + 63, 64)
    above, below = (d, zh * 4 + 4), (d, zh * 4 - 1)

    def at_x(k):
        return (lax.rem(x + k, 4) * 16 + zl * 2 + c, p)

    def at_z(k):
        return (x * 16 + lax.rem(zl + k, 8) * 2 + c, p)

    def at_y(q):
        return (d, zh * 4 + q)

    def send(src, dst, send_sem, recv_sem, device):
        return pltpu.make_async_remote_copy(
            src_ref=src, dst_ref=dst, send_sem=send_sem, recv_sem=recv_sem,
            device_id=device, device_id_type=MESH,
        )

    barrier = pltpu.get_barrier_semaphore()

    def greet(device):
        pl.semaphore_signal(barrier, inc=1, device_id=device, device_id_type=MESH)

    greet((after, p))
    greet((before, p))
    for k in (1, 2, 3):
        greet(at_y(lax.rem(y + k, 4)))
        greet(at_x(k))
    for k in range(1, 8):
        greet(at_z(k))

    @pl.when((y == 0) & falls)
    def _():
        for q in range(4):
            greet((d, zh * 4 - 4 + q))

    @pl.when((y == 3) & rises)
    def _():
        for q in range(4):
            greet((d, zh * 4 + 4 + q))

    def coupling(g, entry):
        rows = slice(g * SPAN, (g + 1) * SPAN)
        total = None
        for k in range(2):
            listed = jnp.full((1, SPAN), blocks_ref[g, k], jnp.int32) == entry
            weight = jnp.where(listed, 1.0, 0.0).astype(BF16)
            part = f_ref[rows, k * SPAN:(k + 1) * SPAN] * weight
            total = part if total is None else total + part
        return total

    def own_block(b):
        return e_ref[b * SPAN:(b + 1) * SPAN, :]

    for g in (1, 2):
        total = mm(coupling(g, g), own_block(g - 1))
        total += mm(coupling(g, g + 1), own_block(g))
        total += mm(coupling(g, g + 2), own_block(g + 1))
        y_ref[g * SPAN:(g + 1) * SPAN, :] = total.astype(BF16)

    w_row = freq_ref[...].astype(F32)
    freq_mine[...] = jnp.broadcast_to(w_row, (8, MODES))

    pl.semaphore_wait(barrier, 15 + lax.div(6 - zh, 4) + lax.div(zh + 3, 4))

    def up_rows(q):
        return e_ref.at[pl.ds(UP_ROWS[q], PART)]

    def down_rows(q):
        return y_ref.at[pl.ds(SPAN + q * PART, PART)]

    def slot(buf, q):
        return buf.at[pl.ds(pl.multiple_of(q * PART, PART), PART)]

    up_far = [
        send(up_rows(q), relay_up, up_s.at[q], relay_r.at[0], at_y(q)) for q in range(3)
    ] + [send(up_rows(3), slot(eprev, 3), up_s.at[3], up_r.at[3], above)]
    down_far = [send(down_rows(0), slot(ynext, 0), down_s.at[0], down_r.at[0], below)] + [
        send(down_rows(q), relay_down, down_s.at[q], relay_r.at[1], at_y(q))
        for q in range(1, 4)
    ]
    up_near = [
        send(up_rows(q), slot(eprev, q), up_s.at[q], up_r.at[q], (d, p + 1)) for q in range(4)
    ]
    down_near = [
        send(down_rows(q), slot(ynext, q), down_s.at[q], down_r.at[q], (d, p - 1))
        for q in range(4)
    ]
    pass_up = send(relay_up, slot(eprev, y), relay_s.at[0], up_r.at[y], above)
    pass_down = send(relay_down, slot(ynext, y), relay_s.at[1], down_r.at[y], below)
    up_is_far, down_is_far = (y == 3) & rises, (y == 0) & falls
    relays_up, relays_down = (y < 3) & rises, (y > 0) & falls

    @pl.when(up_is_far)
    def _():
        for copy in up_far:
            copy.start()

    @pl.when(down_is_far)
    def _():
        for copy in down_far:
            copy.start()

    halo_copies = [
        send(e_ref.at[pl.ds(3 * SPAN, SPAN)], halo.at[0], halo_s.at[0], halo_r.at[0], (after, p)),
        send(e_ref.at[pl.ds(0, SPAN)], halo.at[1], halo_s.at[1], halo_r.at[1], (before, p)),
    ]
    for copy in halo_copies:
        copy.start()
    freq_copy = send(freq_mine, freq_next, freq_sem.at[0], freq_sem.at[1], (d, p - 1))

    @pl.when(has_prev)
    def _():
        freq_copy.start()

    @pl.when(relays_up)
    def _():
        pass_up_in = send(relay_up, relay_up, relay_s.at[0], relay_r.at[0], above)
        pass_up_in.wait_recv()
        pass_up.start()

    @pl.when(relays_down)
    def _():
        pass_down_in = send(relay_down, relay_down, relay_s.at[1], relay_r.at[1], below)
        pass_down_in.wait_recv()
        pass_down.start()

    @pl.when(y < 3)
    def _():
        for copy in up_near:
            copy.start()

    @pl.when(y > 0)
    def _():
        for copy in down_near:
            copy.start()

    for copy in halo_copies:
        copy.wait_recv()
    for g, side, away, near in ((0, 0, 0, 2), (3, 1, 5, 3)):
        total = mm(coupling(g, away), halo[side]) + mm(coupling(g, near), own_block(near - 1))
        y_ref[g * SPAN:(g + 1) * SPAN, :] = total.astype(BF16)

    def fill(m, lefts, rights):
        def tile(i, carry):
            cols = pl.ds(pl.multiple_of(i * 256, 256), 256)
            total = None
            for left, right in zip(lefts, rights):
                part = mtm(left[:, cols], right[...])
                total = part if total is None else total + part
            pairs[m, pl.ds(i * 16, 16)] = total.reshape(16, 2, 8, MODES)
            return carry

        lax.fori_loop(0, 2, tile, 0)

    def core_copy(m):
        return send(
            pairs.at[m, :, 1 - c], core_in.at[m], core_sem.at[0, m], core_sem.at[1, m],
            (d + 1 - 2 * c, p),
        )

    def x_copy(m, k):
        return send(
            x_out.at[m, k - 1], x_in.at[m, k - 1], x_s.at[m, k - 1], x_r.at[m, k - 1], at_x(k)
        )

    def z_copy(m, k):
        return send(
            z_out.at[m, lax.rem(zl + k, 8)], z_in.at[m, k - 1],
            z_s.at[m, k - 1], z_r.at[m, k - 1], at_z(k),
        )

    def after_core(m, xx):
        rows = pl.ds(pl.multiple_of(xx * 8, 8), 8)
        return pairs[m, rows, c] + core_in[m, rows]

    def start_x(m):
        core_copy(m).wait_recv()
        for k in (1, 2, 3):
            value = after_core(m, lax.rem(x + k, 4))
            x_out[m, k - 1] = value.reshape(64, MODES).astype(BF16)
            x_copy(m, k).start()

    def start_z(m):
        total = after_core(m, x)
        for k in (1, 2, 3):
            x_copy(m, k).wait_recv()
            total = total + x_in[m, k - 1].astype(F32).reshape(8, 8, MODES)
        z_out[m] = total
        for k in range(1, 8):
            z_copy(m, k).start()

    def finish(m):
        total = z_out[m, zl]
        for k in range(1, 8):
            z_copy(m, k).wait_recv()
            total = total + z_in[m, k - 1]
        return total

    fill(SELF, (e_ref,), (y_ref,))
    core_copy(SELF).start()
    start_x(SELF)
    start_z(SELF)

    def run_next():
        for q in range(4):
            up = send(slot(ynext, q), slot(ynext, q), down_s.at[q], down_r.at[q], (d, p + 1))
            up.wait_recv()
        fill(NEXT, (e_ref.at[pl.ds(SPAN, 2 * SPAN)],), (ynext,))
        core_copy(NEXT).start()
        start_x(NEXT)
        start_z(NEXT)

    prev_copy = send(prev_out, prev_in, prev_sem.at[0], prev_sem.at[1], (d, p - 1))

    def run_prev():
        for q in range(4):
            up = send(slot(eprev, q), slot(eprev, q), up_s.at[q], up_r.at[q], (d, p - 1))
            up.wait_recv()
        fill(
            PREV,
            (eprev.at[pl.ds(0, SPAN)], eprev.at[pl.ds(SPAN, SPAN)]),
            (y_ref.at[pl.ds(0, SPAN)], y_ref.at[pl.ds(3 * SPAN, SPAN)]),
        )
        core_copy(PREV).start()
        start_x(PREV)
        start_z(PREV)
        prev_out[...] = finish(PREV)
        prev_copy.start()

    @pl.when(y == 3)
    def _():
        run_prev()

    @pl.when(has_next)
    def _():
        run_next()

    @pl.when((y < 3) & has_prev)
    def _():
        run_prev()

    lane = lax.broadcasted_iota(jnp.int32, (8, MODES), 1)
    row = lax.broadcasted_iota(jnp.int32, (8, MODES), 0)

    def window(which):
        tiles = [mask_ref[which, x, j].astype(F32) for j in range(4)]
        return jnp.where(
            lane < 256,
            jnp.where(lane < 128, tiles[0], tiles[1]),
            jnp.where(lane < 384, tiles[2], tiles[3]),
        )

    w_all = freq_mine[...]
    w_mine = jnp.sum(jnp.where(lane == 8 * d + row, w_all, 0.0), axis=1, keepdims=True)
    own_pairs = finish(SELF) * window(0)
    self_ref[0] = own_pairs
    total = jnp.sum(own_pairs * own_pairs * lorentz(w_mine - w_all), axis=1, keepdims=True)
    scale = math.pi / 3.0 / (2.0 * MODES * w_mine * w_mine)
    lane8 = lax.broadcasted_iota(jnp.int32, (8, 128), 1)
    row8 = lax.broadcasted_iota(jnp.int32, (8, 128), 0)

    def put(sums):
        spread = jnp.where(lane8 == row8, sums * scale, 0.0)
        diff_ref[...] = jnp.sum(spread, axis=0, keepdims=True)[:, 0:8]

    @pl.when(has_next)
    def _():
        send(freq_mine, freq_next, freq_sem.at[0], freq_sem.at[1], (d, p + 1)).wait_recv()
        send(prev_out, prev_in, prev_sem.at[0], prev_sem.at[1], (d, p + 1)).wait_recv()
        next_pairs = (finish(NEXT) + prev_in[...]) * window(1)
        next_ref[0] = next_pairs
        ahead = next_pairs * next_pairs * lorentz(w_mine - freq_next[...])
        put(total + jnp.sum(ahead, axis=1, keepdims=True))

    @pl.when(p == 15)
    def _():
        next_ref[0] = jnp.zeros((8, MODES), F32)
        put(total)

    @pl.when(has_next)
    def _():
        for q in range(4):
            up_near[q].wait_send()

    @pl.when(has_prev)
    def _():
        for q in range(4):
            down_near[q].wait_send()
        freq_copy.wait_send()
        prev_copy.wait_send()

    for copy in halo_copies:
        copy.wait_send()

    @pl.when(relays_up)
    def _():
        pass_up.wait_send()

    @pl.when(relays_down)
    def _():
        pass_down.wait_send()

    def drain(m):
        core_copy(m).wait_send()
        for k in (1, 2, 3):
            x_copy(m, k).wait_send()
        for k in range(1, 8):
            z_copy(m, k).wait_send()

    drain(SELF)

    @pl.when(has_next)
    def _():
        drain(NEXT)

    @pl.when(has_prev)
    def _():
        drain(PREV)


def shards(eigvec, flux, blocks, tile_mask, freq):
    vmem = pl.BlockSpec(memory_space=pltpu.VMEM)
    smem = pl.BlockSpec(memory_space=pltpu.SMEM)
    dma = pltpu.SemaphoreType.DMA
    return pl.pallas_call(
        kernel,
        out_shape=(
            jax.ShapeDtypeStruct((1, 8, MODES), F32),
            jax.ShapeDtypeStruct((1, 8, MODES), F32),
            jax.ShapeDtypeStruct((1, 8), F32),
        ),
        in_specs=[vmem, vmem, smem, smem, vmem],
        out_specs=(vmem, vmem, vmem),
        scratch_shapes=[
            pltpu.VMEM((4 * SPAN, MODES), BF16),
            pltpu.VMEM((2, SPAN, MODES), BF16),
            pltpu.VMEM((2 * SPAN, MODES), BF16),
            pltpu.VMEM((2 * SPAN, MODES), BF16),
            pltpu.VMEM((PART, MODES), BF16),
            pltpu.VMEM((PART, MODES), BF16),
            pltpu.VMEM((8, MODES), F32),
            pltpu.VMEM((8, MODES), F32),
            pltpu.VMEM((3, 32, 2, 8, MODES), F32),
            pltpu.VMEM((3, 32, 8, MODES), F32),
            pltpu.VMEM((3, 3, 64, MODES), BF16),
            pltpu.VMEM((3, 3, 64, MODES), BF16),
            pltpu.VMEM((3, 8, 8, MODES), F32),
            pltpu.VMEM((3, 7, 8, MODES), F32),
            pltpu.VMEM((8, MODES), F32),
            pltpu.VMEM((8, MODES), F32),
            dma((2,)), dma((2,)),
            dma((4,)), dma((4,)),
            dma((4,)), dma((4,)),
            dma((2,)), dma((2,)),
            dma((2,)),
            dma((2, 3)),
            dma((3, 3)), dma((3, 3)),
            dma((3, 7)), dma((3, 7)),
            dma((2,)),
        ],
        compiler_params=pltpu.CompilerParams(
            collective_id=0, has_side_effects=True, vmem_limit_bytes=48 << 20
        ),
        cost_estimate=pl.CostEstimate(
            flops=3_000_000_000, bytes_accessed=4_000_000, transcendentals=0
        ),
    )(eigvec, flux, blocks, tile_mask[0], freq)


def solution(mesh):
    return jax.shard_map(
        shards,
        mesh=mesh,
        in_specs=(
            P("domain", "panel"),
            P("domain", None),
            P("domain", None),
            P("panel", None, None, None),
            P("panel", None),
        ),
        out_specs=(P("panel", "domain", None), P("panel", "domain", None), P("panel", "domain")),
        check_vma=False,
    )
```

```python
import math

import jax
import jax.numpy as jnp
from jax import lax
from jax.experimental import pallas as pl
from jax.experimental.pallas import tpu as pltpu
from jax.sharding import PartitionSpec as P

MESH = pl.DeviceIdType.MESH
F32 = jnp.float32
BF16 = jnp.bfloat16

WIDTH = 0.25
SPAN = 384
MODES = 512
PART = 192
LANES = 128
SELF, NEAR, FAR = 0, 1, 2


def lorentz(gap):
    return WIDTH / math.pi / (gap * gap + WIDTH * WIDTH)


def mm(a, b):
    return jnp.dot(a, b, preferred_element_type=F32)


def mtm(a, b):
    return lax.dot_general(a, b, (((0,), (0,)), ((), ())), preferred_element_type=F32)


def chunk(k):
    return pl.ds(pl.multiple_of(k * LANES, LANES), LANES)


def kernel(
    e_in, f_in, blocks_in, mask_in, freq_in,
    self_ref, next_ref, diff_ref,
    e_ref, f_ref, blocks_ref, mask_ref, freq_ref,
    y_ref, halo, eprev, ynext, relay_up, relay_down, freq_mine, freq_next, next_sum,
    pairs, core_in, x_out, x_in, z_own, z_out, z_in, piece_out, piece_in,
    load_sem, halo_s, halo_r, up_s, up_r, down_s, down_r, relay_s, relay_r, freq_sem,
    core_s, core_r, x_s, x_r, z_s, z_r, piece_sem, ready,
):
    d = lax.axis_index("domain")
    p = lax.axis_index("panel")
    x, zl, c = d // 16, lax.rem(d // 2, 8), lax.rem(d, 2)
    y, zh = lax.rem(p, 4), p // 4
    has_next, has_prev = p < 15, p > 0
    rises, falls = zh < 3, zh > 0
    after, before = lax.rem(d + 1, 64), lax.rem(d + 63, 64)
    above, below = (d, zh * 4 + 4), (d, zh * 4 - 1)

    loads = [
        pltpu.make_async_copy(src, dst, load_sem.at[i])
        for i, (src, dst) in enumerate(
            ((e_in, e_ref), (f_in, f_ref), (blocks_in, blocks_ref), (freq_in, freq_ref), (mask_in, mask_ref))
        )
    ]
    for load in loads:
        load.start()

    def at_x(k):
        return (lax.rem(x + k, 4) * 16 + zl * 2 + c, p)

    def at_z(k):
        return (x * 16 + lax.rem(zl + k, 8) * 2 + c, p)

    def at_y(q):
        return (d, zh * 4 + q)

    def send(src, dst, send_sem, recv_sem, device):
        return pltpu.make_async_remote_copy(
            src_ref=src, dst_ref=dst, send_sem=send_sem, recv_sem=recv_sem,
            device_id=device, device_id_type=MESH,
        )

    barrier = pltpu.get_barrier_semaphore()

    def greet(device):
        pl.semaphore_signal(barrier, inc=1, device_id=device, device_id_type=MESH)

    @pl.when((y == 3) & rises)
    def _():
        for q in range(4):
            greet((d, zh * 4 + 4 + q))

    @pl.when((y < 3) & rises)
    def _():
        greet(above)

    for k in range(1, 8):
        greet(at_z(k))
    greet((after, p))
    greet((before, p))
    for k in (1, 2, 3):
        greet(at_y(lax.rem(y + k, 4)))
        greet(at_x(k))

    def coupling(g, entry):
        rows = slice(g * SPAN, (g + 1) * SPAN)
        total = None
        for k in range(2):
            listed = jnp.full((1, SPAN), blocks_ref[k, g], jnp.int32) == entry
            weight = jnp.where(listed, 1.0, 0.0).astype(BF16)
            part = f_ref[rows, k * SPAN:(k + 1) * SPAN] * weight
            total = part if total is None else total + part
        return total

    def own_block(b):
        return e_ref[b * SPAN:(b + 1) * SPAN, :]

    for load in loads:
        load.wait()
    for g in (1, 2):
        total = mm(coupling(g, g), own_block(g - 1))
        total += mm(coupling(g, g + 1), own_block(g))
        total += mm(coupling(g, g + 2), own_block(g + 1))
        y_ref[g * SPAN:(g + 1) * SPAN, :] = total.astype(BF16)

    freq_mine[...] = jnp.broadcast_to(freq_ref[...].astype(F32), (8, MODES))

    from_below = lax.div(zh + 3, 4) * (1 + 3 * lax.div(3 - y, 3))
    pl.semaphore_wait(barrier, 15 + from_below)

    @pl.when((y == 0) & falls)
    def _():
        for q in range(4):
            pl.semaphore_signal(
                ready, inc=1, device_id=(d, zh * 4 - 4 + q), device_id_type=MESH
            )

    def quarter(buf, q, k):
        return buf.at[pl.ds(pl.multiple_of(q * PART, PART), PART), chunk(k)]

    def up_part(q, k):
        start = q * PART + lax.div(q, 2) * (2 * SPAN)
        return e_ref.at[pl.ds(pl.multiple_of(start, PART), PART), chunk(k)]

    def down_part(q, k):
        return y_ref.at[pl.ds(pl.multiple_of(SPAN + q * PART, PART), PART), chunk(k)]

    def up(q, k, device):
        return send(up_part(q, k), quarter(eprev, q, k), up_s.at[q, k], up_r.at[q, k], device)

    def down(q, k, device):
        return send(
            down_part(q, k), quarter(ynext, q, k), down_s.at[q, k], down_r.at[q, k], device
        )

    def to_relay_up(q, k):
        return send(
            up_part(q, k), relay_up.at[:, chunk(k)], up_s.at[q, k], relay_r.at[0, k], at_y(q)
        )

    def to_relay_down(q, k):
        return send(
            down_part(q, k), relay_down.at[:, chunk(k)], down_s.at[q, k], relay_r.at[1, k], at_y(q)
        )

    def pass_up(k):
        return send(
            relay_up.at[:, chunk(k)], quarter(eprev, y, k), relay_s.at[0, k], up_r.at[y, k], above
        )

    def pass_down(k):
        return send(
            relay_down.at[:, chunk(k)], quarter(ynext, y, k),
            relay_s.at[1, k], down_r.at[y, k], below,
        )

    halo_copies = [
        send(e_ref.at[pl.ds(3 * SPAN, SPAN)], halo.at[0], halo_s.at[0], halo_r.at[0], (after, p)),
        send(e_ref.at[pl.ds(0, SPAN)], halo.at[1], halo_s.at[1], halo_r.at[1], (before, p)),
    ]
    for copy in halo_copies:
        copy.start()

    @pl.when((y == 3) & rises)
    def _():
        @pl.loop(0, 4)
        def _(k):
            for q in (2, 0, 1):
                to_relay_up(q, k).start()

    @pl.when((y == 0) & falls)
    def _():
        @pl.loop(0, 4)
        def _(k):
            for q in (1, 3, 2):
                to_relay_down(q, k).start()

    freq_copy = send(freq_mine, freq_next, freq_sem.at[0], freq_sem.at[1], (d, p - 1))

    @pl.when(has_prev)
    def _():
        freq_copy.start()

    relays_up, relays_down = (y < 3) & rises, (y > 0) & falls

    @pl.loop(0, 4)
    def _(k):
        @pl.when(y < 3)
        def _():
            for q in range(4):
                up(q, k, (d, p + 1)).start()

        @pl.when(y > 0)
        def _():
            for q in range(4):
                down(q, k, (d, p - 1)).start()

    def cross_up():
        @pl.when(rises)
        def _():
            pl.semaphore_wait(ready, 1)

        @pl.when((y == 3) & rises)
        def _():
            @pl.loop(0, 4)
            def _(k):
                up(3, k, above).start()

        @pl.when(relays_up)
        def _():
            @pl.loop(0, 4)
            def _(k):
                send(
                    relay_up.at[:, chunk(k)], relay_up.at[:, chunk(k)],
                    relay_s.at[0, k], relay_r.at[0, k], above,
                ).wait_recv()
                pass_up(k).start()

    def cross_down():
        @pl.when((y == 0) & falls)
        def _():
            @pl.loop(0, 4)
            def _(k):
                down(0, k, below).start()

        @pl.when(relays_down)
        def _():
            @pl.loop(0, 4)
            def _(k):
                send(
                    relay_down.at[:, chunk(k)], relay_down.at[:, chunk(k)],
                    relay_s.at[1, k], relay_r.at[1, k], below,
                ).wait_recv()
                pass_down(k).start()

    for copy in halo_copies:
        copy.wait_recv()

    pl.when(zl < 4)(cross_up)
    pl.when(zl >= 4)(cross_down)

    for g, side, away, near in ((0, 0, 0, 2), (3, 1, 5, 3)):
        total = mm(coupling(g, away), halo[side]) + mm(coupling(g, near), own_block(near - 1))
        y_ref[g * SPAN:(g + 1) * SPAN, :] = total.astype(BF16)

    other_core = (d + 1 - 2 * c, p)

    def fill(m, lefts, rights):
        @pl.loop(0, 2)
        def _(i):
            cols = pl.ds(pl.multiple_of(i * 256, 256), 256)
            total = None
            for left, right in zip(lefts, rights):
                part = mtm(left[:, cols], right[...])
                total = part if total is None else total + part
            pairs[m, pl.ds(i * 16, 16)] = total.reshape(16, 2, 8, MODES)

    def core_copy(m):
        return send(
            pairs.at[m, :, 1 - c], core_in.at[m], core_s.at[m], core_r.at[m], other_core
        )

    def x_copy(m, k):
        return send(
            x_out.at[m, k - 1], x_in.at[m, k - 1], x_s.at[m, k - 1], x_r.at[m, k - 1], at_x(k)
        )

    def z_copy(m, k):
        return send(
            z_out.at[m, lax.rem(zl + k, 8)], z_in.at[m, k - 1],
            z_s.at[m, k - 1], z_r.at[m, k - 1], at_z(k),
        )

    def after_core(m, xx):
        rows = pl.ds(pl.multiple_of(xx * 8, 8), 8)
        return pairs[m, rows, c] + core_in[m, rows]

    def start_x(m):
        core_copy(m).wait_recv()
        for k in (1, 2, 3):
            value = after_core(m, lax.rem(x + k, 4))
            x_out[m, k - 1] = value.reshape(64, MODES).astype(BF16)
            x_copy(m, k).start()

    def start_z(m):
        total = after_core(m, x)
        for k in (1, 2, 3):
            x_copy(m, k).wait_recv()
            total = total + x_in[m, k - 1].astype(F32).reshape(8, 8, MODES)
        z_own[m] = total
        halves = jnp.concatenate([total[:, :, :256], total[:, :, 256:]], axis=1)
        z_out[m] = halves.astype(BF16)
        for k in range(1, 8):
            z_copy(m, k).start()

    def finish(m):
        for k in range(1, 8):
            z_copy(m, k).wait_recv()
        arrived = z_in[m, 0].astype(F32)
        for k in range(2, 8):
            arrived = arrived + z_in[m, k - 1].astype(F32)
        return z_own[m, zl] + jnp.concatenate([arrived[:8], arrived[8:]], axis=1)

    def await_up(k):
        for q in range(4):
            send(
                quarter(eprev, q, k), quarter(eprev, q, k), up_s.at[q, k], up_r.at[q, k], (d, p - 1)
            ).wait_recv()

    def await_down(k):
        for q in range(4):
            send(
                quarter(ynext, q, k), quarter(ynext, q, k),
                down_s.at[q, k], down_r.at[q, k], (d, p + 1),
            ).wait_recv()

    inner_e = e_ref.at[pl.ds(SPAN, 2 * SPAN)]
    prev_pair = (
        (eprev.at[pl.ds(0, SPAN)], eprev.at[pl.ds(SPAN, SPAN)]),
        (y_ref.at[pl.ds(0, SPAN)], y_ref.at[pl.ds(3 * SPAN, SPAN)]),
    )
    def piece_copy(device):
        return send(piece_out, piece_in, piece_sem.at[0], piece_sem.at[1], device)

    def next_part():
        for k in range(4):
            await_down(k)
        return (inner_e,), (ynext,)

    def prev_part():
        for k in range(4):
            await_up(k)
        return prev_pair

    fill(SELF, (e_ref,), (y_ref,))
    core_copy(SELF).start()
    start_x(SELF)
    start_z(SELF)
    pl.when(zl >= 4)(cross_up)
    pl.when(zl < 4)(cross_down)

    @pl.when(y == 3)
    def _():
        fill(NEAR, *prev_part())

    @pl.when(y < 3)
    def _():
        fill(NEAR, *next_part())

    core_copy(NEAR).start()
    start_x(NEAR)
    start_z(NEAR)
    has_far = jnp.logical_or((y == 3) & rises, (y < 3) & has_prev)

    @pl.when((y == 3) & rises)
    def _():
        fill(FAR, *next_part())

    @pl.when((y < 3) & has_prev)
    def _():
        fill(FAR, *prev_part())

    @pl.when(has_far)
    def _():
        core_copy(FAR).start()
        start_x(FAR)
        start_z(FAR)

    @pl.when((y == 3) & rises)
    def _():
        next_sum[...] = finish(FAR)

    @pl.when((y < 3) & has_prev)
    def _():
        piece_out[...] = finish(FAR)
        piece_copy((d, p - 1)).start()

    near = finish(NEAR)

    @pl.when(y == 3)
    def _():
        piece_out[...] = near
        piece_copy((d, p - 1)).start()

    @pl.when(y < 3)
    def _():
        next_sum[...] = near

    lane = lax.broadcasted_iota(jnp.int32, (8, MODES), 1)
    row = lax.broadcasted_iota(jnp.int32, (8, MODES), 0)

    def window(which):
        tiles = [mask_ref[0, which, x, j].astype(F32) for j in range(4)]
        return jnp.where(
            lane < 256,
            jnp.where(lane < 128, tiles[0], tiles[1]),
            jnp.where(lane < 384, tiles[2], tiles[3]),
        )

    w_all = freq_mine[...]
    w_mine = jnp.sum(jnp.where(lane == 8 * d + row, w_all, 0.0), axis=1, keepdims=True)
    own_pairs = finish(SELF) * window(0)
    self_ref[0] = own_pairs
    total = jnp.sum(own_pairs * own_pairs * lorentz(w_mine - w_all), axis=1, keepdims=True)
    scale = math.pi / 3.0 / (2.0 * MODES * w_mine * w_mine)
    lane8 = lax.broadcasted_iota(jnp.int32, (8, 128), 1)
    row8 = lax.broadcasted_iota(jnp.int32, (8, 128), 0)

    def put(sums):
        spread = jnp.where(lane8 == row8, sums * scale, 0.0)
        diff_ref[...] = jnp.sum(spread, axis=0, keepdims=True)[:, 0:8]

    @pl.when(has_next)
    def _():
        send(freq_mine, freq_next, freq_sem.at[0], freq_sem.at[1], (d, p + 1)).wait_recv()
        weights = lorentz(w_mine - freq_next[...])
        piece_copy((d, p + 1)).wait_recv()
        next_pairs = (next_sum[...] + piece_in[...]) * window(1)
        next_ref[0] = next_pairs
        put(total + jnp.sum(next_pairs * next_pairs * weights, axis=1, keepdims=True))

    @pl.when(p == 15)
    def _():
        next_ref[0] = jnp.zeros((8, MODES), F32)
        put(total)

    @pl.loop(0, 4)
    def _(k):
        @pl.when(has_next)
        def _():
            for q in range(4):
                up(q, k, above).wait_send()

        @pl.when(has_prev)
        def _():
            for q in range(4):
                down(q, k, below).wait_send()

        @pl.when(relays_up)
        def _():
            pass_up(k).wait_send()

        @pl.when(relays_down)
        def _():
            pass_down(k).wait_send()

    @pl.when(has_prev)
    def _():
        freq_copy.wait_send()
        piece_copy((d, p - 1)).wait_send()

    for copy in halo_copies:
        copy.wait_send()

    def drain(m):
        core_copy(m).wait_send()
        for k in (1, 2, 3):
            x_copy(m, k).wait_send()
        for k in range(1, 8):
            z_copy(m, k).wait_send()

    drain(SELF)
    drain(NEAR)

    @pl.when(has_far)
    def _():
        drain(FAR)


def hand_out(a_ref, b_ref, c_ref, self_ref, next_ref, diff_ref):
    self_ref[...] = a_ref[...]
    next_ref[...] = b_ref[...]
    diff_ref[...] = c_ref[...]


def shards(eigvec, flux, blocks, tile_mask, freq):
    vmem = pl.BlockSpec(memory_space=pltpu.VMEM)
    hbm = pl.BlockSpec(memory_space=pltpu.MemorySpace.HBM)
    dma = pltpu.SemaphoreType.DMA
    sums = pl.pallas_call(
        kernel,
        out_shape=(
            jax.ShapeDtypeStruct((1, 8, MODES), F32),
            jax.ShapeDtypeStruct((1, 8, MODES), F32),
            jax.ShapeDtypeStruct((1, 8), F32),
        ),
        in_specs=[hbm] * 5,
        out_specs=(vmem, vmem, vmem),
        scratch_shapes=[
            pltpu.VMEM((4 * SPAN, MODES), BF16),
            pltpu.VMEM((4 * SPAN, 2 * SPAN), BF16),
            pltpu.SMEM((2, 4), jnp.int32),
            pltpu.SMEM((1, 2, 4, 4), jnp.int32),
            pltpu.VMEM((1, MODES), BF16),
            pltpu.VMEM((4 * SPAN, MODES), BF16),
            pltpu.VMEM((2, SPAN, MODES), BF16),
            pltpu.VMEM((2 * SPAN, MODES), BF16),
            pltpu.VMEM((2 * SPAN, MODES), BF16),
            pltpu.VMEM((PART, MODES), BF16),
            pltpu.VMEM((PART, MODES), BF16),
            pltpu.VMEM((8, MODES), F32),
            pltpu.VMEM((8, MODES), F32),
            pltpu.VMEM((8, MODES), F32),
            pltpu.VMEM((3, 32, 2, 8, MODES), F32),
            pltpu.VMEM((3, 32, 8, MODES), F32),
            pltpu.VMEM((3, 3, 64, MODES), BF16),
            pltpu.VMEM((3, 3, 64, MODES), BF16),
            pltpu.VMEM((3, 8, 8, MODES), F32),
            pltpu.VMEM((3, 8, 16, 256), BF16),
            pltpu.VMEM((3, 7, 16, 256), BF16),
            pltpu.VMEM((8, MODES), F32),
            pltpu.VMEM((8, MODES), F32),
            dma((5,)),
            dma((2,)), dma((2,)),
            dma((4, 4)), dma((4, 4)),
            dma((4, 4)), dma((4, 4)),
            dma((2, 4)), dma((2, 4)),
            dma((2,)),
            dma((3,)), dma((3,)),
            dma((3, 3)), dma((3, 3)),
            dma((3, 7)), dma((3, 7)),
            dma((2,)),
            pltpu.SemaphoreType.REGULAR,
        ],
        compiler_params=pltpu.CompilerParams(
            collective_id=0, has_side_effects=True, vmem_limit_bytes=62 << 20
        ),
        cost_estimate=pl.CostEstimate(
            flops=3_000_000_000, bytes_accessed=4_000_000, transcendentals=0
        ),
    )(eigvec, flux, blocks.T, tile_mask, freq)
    return pl.pallas_call(
        hand_out,
        out_shape=tuple(jax.ShapeDtypeStruct(v.shape, v.dtype) for v in sums),
        in_specs=[vmem] * 3,
        out_specs=(vmem, vmem, vmem),
    )(*sums)


def solution(mesh):
    return jax.shard_map(
        shards,
        mesh=mesh,
        in_specs=(
            P("domain", "panel"),
            P("domain", None),
            P("domain", None),
            P("panel", None, None, None),
            P("panel", None),
        ),
        out_specs=(P("panel", "domain", None), P("panel", "domain", None), P("panel", "domain")),
        check_vma=False,
    )
```

```python
import math

import jax
import jax.numpy as jnp
from jax import lax
from jax.experimental import pallas as pl
from jax.experimental.pallas import tpu as pltpu
from jax.sharding import PartitionSpec as P

MESH = pl.DeviceIdType.MESH
F32 = jnp.float32
BF16 = jnp.bfloat16

WIDTH = 0.25
SPAN = 384
MODES = 512
PART = 192
LANES = 128
SELF, NEAR, FAR = 0, 1, 2


def lorentz(gap):
    return WIDTH / math.pi / (gap * gap + WIDTH * WIDTH)


def mm(a, b):
    return jnp.dot(a, b, preferred_element_type=F32)


def mtm(a, b):
    return lax.dot_general(a, b, (((0,), (0,)), ((), ())), preferred_element_type=F32)


def chunk(k):
    return pl.ds(pl.multiple_of(k * LANES, LANES), LANES)


def kernel(
    e_in, f_in, blocks_in, mask_in, freq_in,
    self_ref, next_ref, diff_ref,
    e_ref, f_ref, blocks_ref, mask_ref, freq_ref,
    y_ref, halo, eprev, ynext, relay_up, relay_down, freq_mine, freq_next, next_sum,
    pairs, core_in, x_out, x_in, z_own, z_out, z_in, piece_out, piece_in,
    load_sem, halo_s, halo_r, up_s, up_r, down_s, down_r, relay_s, relay_r, freq_sem,
    core_s, core_r, x_s, x_r, z_s, z_r, piece_sem, ready,
):
    d = lax.axis_index("domain")
    p = lax.axis_index("panel")
    x, zl, c = d // 16, lax.rem(d // 2, 8), lax.rem(d, 2)
    y, zh = lax.rem(p, 4), p // 4
    has_next, has_prev = p < 15, p > 0
    rises, falls = zh < 3, zh > 0
    after, before = lax.rem(d + 1, 64), lax.rem(d + 63, 64)
    above, below = (d, zh * 4 + 4), (d, zh * 4 - 1)

    loads = [
        pltpu.make_async_copy(src, dst, load_sem.at[i])
        for i, (src, dst) in enumerate(
            ((e_in, e_ref), (f_in, f_ref), (blocks_in, blocks_ref), (freq_in, freq_ref), (mask_in, mask_ref))
        )
    ]
    for load in loads:
        load.start()

    def at_x(k):
        return (lax.rem(x + k, 4) * 16 + zl * 2 + c, p)

    def at_z(k):
        return (x * 16 + lax.rem(zl + k, 8) * 2 + c, p)

    def at_y(q):
        return (d, zh * 4 + q)

    def send(src, dst, send_sem, recv_sem, device):
        return pltpu.make_async_remote_copy(
            src_ref=src, dst_ref=dst, send_sem=send_sem, recv_sem=recv_sem,
            device_id=device, device_id_type=MESH,
        )

    barrier = pltpu.get_barrier_semaphore()

    def greet(device):
        pl.semaphore_signal(barrier, inc=1, device_id=device, device_id_type=MESH)

    @pl.when((y == 3) & rises)
    def _():
        for q in range(4):
            greet((d, zh * 4 + 4 + q))

    @pl.when((y < 3) & rises)
    def _():
        greet(above)

    for k in range(1, 8):
        greet(at_z(k))
    greet((after, p))
    greet((before, p))
    for k in (1, 2, 3):
        greet(at_y(lax.rem(y + k, 4)))
        greet(at_x(k))

    def coupling(g, entry):
        rows = slice(g * SPAN, (g + 1) * SPAN)
        total = None
        for k in range(2):
            listed = jnp.full((1, SPAN), blocks_ref[k, g], jnp.int32) == entry
            weight = jnp.where(listed, 1.0, 0.0).astype(BF16)
            part = f_ref[rows, k * SPAN:(k + 1) * SPAN] * weight
            total = part if total is None else total + part
        return total

    def own_block(b):
        return e_ref[b * SPAN:(b + 1) * SPAN, :]

    for load in loads:
        load.wait()
    for g in (1, 2):
        total = mm(coupling(g, g), own_block(g - 1))
        total += mm(coupling(g, g + 1), own_block(g))
        total += mm(coupling(g, g + 2), own_block(g + 1))
        y_ref[g * SPAN:(g + 1) * SPAN, :] = total.astype(BF16)

    freq_mine[...] = jnp.broadcast_to(freq_ref[...].astype(F32), (8, MODES))

    from_below = lax.div(zh + 3, 4) * (1 + 3 * lax.div(3 - y, 3))
    pl.semaphore_wait(barrier, 15 + from_below)

    @pl.when((y == 0) & falls)
    def _():
        for q in range(4):
            pl.semaphore_signal(
                ready, inc=1, device_id=(d, zh * 4 - 4 + q), device_id_type=MESH
            )

    def quarter(buf, q, k):
        return buf.at[pl.ds(pl.multiple_of(q * PART, PART), PART), chunk(k)]

    def up_part(q, k):
        start = q * PART + lax.div(q, 2) * (2 * SPAN)
        return e_ref.at[pl.ds(pl.multiple_of(start, PART), PART), chunk(k)]

    def down_part(q, k):
        return y_ref.at[pl.ds(pl.multiple_of(SPAN + q * PART, PART), PART), chunk(k)]

    def up(q, k, device):
        return send(up_part(q, k), quarter(eprev, q, k), up_s.at[q, k], up_r.at[q, k], device)

    def down(q, k, device):
        return send(
            down_part(q, k), quarter(ynext, q, k), down_s.at[q, k], down_r.at[q, k], device
        )

    def to_relay_up(q, k):
        return send(
            up_part(q, k), relay_up.at[:, chunk(k)], up_s.at[q, k], relay_r.at[0, k], at_y(q)
        )

    def to_relay_down(q, k):
        return send(
            down_part(q, k), relay_down.at[:, chunk(k)], down_s.at[q, k], relay_r.at[1, k], at_y(q)
        )

    def pass_up(k):
        return send(
            relay_up.at[:, chunk(k)], quarter(eprev, y, k), relay_s.at[0, k], up_r.at[y, k], above
        )

    def pass_down(k):
        return send(
            relay_down.at[:, chunk(k)], quarter(ynext, y, k),
            relay_s.at[1, k], down_r.at[y, k], below,
        )

    halo_copies = [
        send(e_ref.at[pl.ds(3 * SPAN, SPAN)], halo.at[0], halo_s.at[0], halo_r.at[0], (after, p)),
        send(e_ref.at[pl.ds(0, SPAN)], halo.at[1], halo_s.at[1], halo_r.at[1], (before, p)),
    ]
    for copy in halo_copies:
        copy.start()

    @pl.when((y == 3) & rises)
    def _():
        @pl.loop(0, 4)
        def _(k):
            for q in (2, 0, 1):
                to_relay_up(q, k).start()

    @pl.when((y == 0) & falls)
    def _():
        @pl.loop(0, 4)
        def _(k):
            for q in (1, 3, 2):
                to_relay_down(q, k).start()

    freq_copy = send(freq_mine, freq_next, freq_sem.at[0], freq_sem.at[1], (d, p - 1))

    @pl.when(has_prev)
    def _():
        freq_copy.start()

    relays_up, relays_down = (y < 3) & rises, (y > 0) & falls

    @pl.loop(0, 4)
    def _(k):
        @pl.when(y < 3)
        def _():
            for q in range(4):
                up(q, k, (d, p + 1)).start()

        @pl.when(y > 0)
        def _():
            for q in range(4):
                down(q, k, (d, p - 1)).start()

    def cross_up():
        @pl.when(rises)
        def _():
            pl.semaphore_wait(ready, 1)

        @pl.when((y == 3) & rises)
        def _():
            @pl.loop(0, 4)
            def _(k):
                up(3, k, above).start()

        @pl.when(relays_up)
        def _():
            @pl.loop(0, 4)
            def _(k):
                send(
                    relay_up.at[:, chunk(k)], relay_up.at[:, chunk(k)],
                    relay_s.at[0, k], relay_r.at[0, k], above,
                ).wait_recv()
                pass_up(k).start()

    def cross_down():
        @pl.when((y == 0) & falls)
        def _():
            @pl.loop(0, 4)
            def _(k):
                down(0, k, below).start()

        @pl.when(relays_down)
        def _():
            @pl.loop(0, 4)
            def _(k):
                send(
                    relay_down.at[:, chunk(k)], relay_down.at[:, chunk(k)],
                    relay_s.at[1, k], relay_r.at[1, k], below,
                ).wait_recv()
                pass_down(k).start()

    pl.when(zh == 0)(cross_up)
    pl.when((zh == 1) & (zl >= 4))(cross_down)
    for copy in halo_copies:
        copy.wait_recv()

    pl.when((zh > 0) & (zl < 4))(cross_up)
    pl.when((zh > 1) & (zl >= 4))(cross_down)

    for g, side, away, near in ((0, 0, 0, 2), (3, 1, 5, 3)):
        total = mm(coupling(g, away), halo[side]) + mm(coupling(g, near), own_block(near - 1))
        y_ref[g * SPAN:(g + 1) * SPAN, :] = total.astype(BF16)

    other_core = (d + 1 - 2 * c, p)

    def fill(m, lefts, rights):
        @pl.loop(0, 2)
        def _(i):
            cols = pl.ds(pl.multiple_of(i * 256, 256), 256)
            total = None
            for left, right in zip(lefts, rights):
                part = mtm(left[:, cols], right[...])
                total = part if total is None else total + part
            pairs[m, pl.ds(i * 16, 16)] = total.reshape(16, 2, 8, MODES)

    def core_copy(m):
        return send(
            pairs.at[m, :, 1 - c], core_in.at[m], core_s.at[m], core_r.at[m], other_core
        )

    def x_copy(m, k):
        return send(
            x_out.at[m, k - 1], x_in.at[m, k - 1], x_s.at[m, k - 1], x_r.at[m, k - 1], at_x(k)
        )

    def z_copy(m, k):
        return send(
            z_out.at[m, lax.rem(zl + k, 8)], z_in.at[m, k - 1],
            z_s.at[m, k - 1], z_r.at[m, k - 1], at_z(k),
        )

    def after_core(m, xx):
        rows = pl.ds(pl.multiple_of(xx * 8, 8), 8)
        return pairs[m, rows, c] + core_in[m, rows]

    def start_x(m):
        core_copy(m).wait_recv()
        for k in (1, 2, 3):
            value = after_core(m, lax.rem(x + k, 4))
            x_out[m, k - 1] = value.reshape(64, MODES).astype(BF16)
            x_copy(m, k).start()

    def start_z(m):
        total = after_core(m, x)
        for k in (1, 2, 3):
            x_copy(m, k).wait_recv()
            total = total + x_in[m, k - 1].astype(F32).reshape(8, 8, MODES)
        z_own[m] = total
        halves = jnp.concatenate([total[:, :, :256], total[:, :, 256:]], axis=1)
        z_out[m] = halves.astype(BF16)
        for k in range(1, 8):
            z_copy(m, k).start()

    def finish(m):
        for k in range(1, 8):
            z_copy(m, k).wait_recv()
        arrived = z_in[m, 0].astype(F32)
        for k in range(2, 8):
            arrived = arrived + z_in[m, k - 1].astype(F32)
        return z_own[m, zl] + jnp.concatenate([arrived[:8], arrived[8:]], axis=1)

    def await_up(k):
        for q in range(4):
            send(
                quarter(eprev, q, k), quarter(eprev, q, k), up_s.at[q, k], up_r.at[q, k], (d, p - 1)
            ).wait_recv()

    def await_down(k):
        for q in range(4):
            send(
                quarter(ynext, q, k), quarter(ynext, q, k),
                down_s.at[q, k], down_r.at[q, k], (d, p + 1),
            ).wait_recv()

    inner_e = e_ref.at[pl.ds(SPAN, 2 * SPAN)]
    prev_pair = (
        (eprev.at[pl.ds(0, SPAN)], eprev.at[pl.ds(SPAN, SPAN)]),
        (y_ref.at[pl.ds(0, SPAN)], y_ref.at[pl.ds(3 * SPAN, SPAN)]),
    )
    def piece_copy(device):
        return send(piece_out, piece_in, piece_sem.at[0], piece_sem.at[1], device)

    def next_part():
        for k in range(4):
            await_down(k)
        return (inner_e,), (ynext,)

    def prev_part():
        for k in range(4):
            await_up(k)
        return prev_pair

    fill(SELF, (e_ref,), (y_ref,))
    core_copy(SELF).start()
    pl.when((zh == 1) & (zl < 4))(cross_down)
    start_x(SELF)
    pl.when((zh > 0) & (zl >= 4))(cross_up)
    pl.when((zh > 1) & (zl < 4))(cross_down)
    start_z(SELF)

    @pl.when(y == 3)
    def _():
        fill(NEAR, *prev_part())

    @pl.when(y < 3)
    def _():
        fill(NEAR, *next_part())

    core_copy(NEAR).start()
    start_x(NEAR)
    start_z(NEAR)
    has_far = jnp.logical_or((y == 3) & rises, (y < 3) & has_prev)

    @pl.when((y == 3) & rises)
    def _():
        fill(FAR, *next_part())

    @pl.when((y < 3) & has_prev)
    def _():
        fill(FAR, *prev_part())

    @pl.when(has_far)
    def _():
        core_copy(FAR).start()
        start_x(FAR)
        start_z(FAR)

    @pl.when((y == 3) & rises)
    def _():
        next_sum[...] = finish(FAR)

    @pl.when((y < 3) & has_prev)
    def _():
        piece_out[...] = finish(FAR)
        piece_copy((d, p - 1)).start()

    near = finish(NEAR)

    @pl.when(y == 3)
    def _():
        piece_out[...] = near
        piece_copy((d, p - 1)).start()

    @pl.when(y < 3)
    def _():
        next_sum[...] = near

    lane = lax.broadcasted_iota(jnp.int32, (8, MODES), 1)
    row = lax.broadcasted_iota(jnp.int32, (8, MODES), 0)

    def window(which):
        tiles = [mask_ref[0, which, x, j].astype(F32) for j in range(4)]
        return jnp.where(
            lane < 256,
            jnp.where(lane < 128, tiles[0], tiles[1]),
            jnp.where(lane < 384, tiles[2], tiles[3]),
        )

    w_all = freq_mine[...]
    w_mine = jnp.sum(jnp.where(lane == 8 * d + row, w_all, 0.0), axis=1, keepdims=True)
    own_pairs = finish(SELF) * window(0)
    self_ref[0] = own_pairs
    total = jnp.sum(own_pairs * own_pairs * lorentz(w_mine - w_all), axis=1, keepdims=True)
    scale = math.pi / 3.0 / (2.0 * MODES * w_mine * w_mine)
    lane8 = lax.broadcasted_iota(jnp.int32, (8, 128), 1)
    row8 = lax.broadcasted_iota(jnp.int32, (8, 128), 0)

    def put(sums):
        spread = jnp.where(lane8 == row8, sums * scale, 0.0)
        diff_ref[...] = jnp.sum(spread, axis=0, keepdims=True)[:, 0:8]

    @pl.when(has_next)
    def _():
        send(freq_mine, freq_next, freq_sem.at[0], freq_sem.at[1], (d, p + 1)).wait_recv()
        weights = lorentz(w_mine - freq_next[...])
        piece_copy((d, p + 1)).wait_recv()
        next_pairs = (next_sum[...] + piece_in[...]) * window(1)
        next_ref[0] = next_pairs
        put(total + jnp.sum(next_pairs * next_pairs * weights, axis=1, keepdims=True))

    @pl.when(p == 15)
    def _():
        next_ref[0] = jnp.zeros((8, MODES), F32)
        put(total)

    @pl.loop(0, 4)
    def _(k):
        @pl.when(has_next)
        def _():
            for q in range(4):
                up(q, k, above).wait_send()

        @pl.when(has_prev)
        def _():
            for q in range(4):
                down(q, k, below).wait_send()

        @pl.when(relays_up)
        def _():
            pass_up(k).wait_send()

        @pl.when(relays_down)
        def _():
            pass_down(k).wait_send()

    @pl.when(has_prev)
    def _():
        freq_copy.wait_send()
        piece_copy((d, p - 1)).wait_send()

    for copy in halo_copies:
        copy.wait_send()

    def drain(m):
        core_copy(m).wait_send()
        for k in (1, 2, 3):
            x_copy(m, k).wait_send()
        for k in range(1, 8):
            z_copy(m, k).wait_send()

    drain(SELF)
    drain(NEAR)

    @pl.when(has_far)
    def _():
        drain(FAR)


def hand_out(a_ref, b_ref, c_ref, self_ref, next_ref, diff_ref):
    self_ref[...] = a_ref[...]
    next_ref[...] = b_ref[...]
    diff_ref[...] = c_ref[...]


def shards(eigvec, flux, blocks, tile_mask, freq):
    vmem = pl.BlockSpec(memory_space=pltpu.VMEM)
    hbm = pl.BlockSpec(memory_space=pltpu.MemorySpace.HBM)
    dma = pltpu.SemaphoreType.DMA
    sums = pl.pallas_call(
        kernel,
        out_shape=(
            jax.ShapeDtypeStruct((1, 8, MODES), F32),
            jax.ShapeDtypeStruct((1, 8, MODES), F32),
            jax.ShapeDtypeStruct((1, 8), F32),
        ),
        in_specs=[hbm] * 5,
        out_specs=(vmem, vmem, vmem),
        scratch_shapes=[
            pltpu.VMEM((4 * SPAN, MODES), BF16),
            pltpu.VMEM((4 * SPAN, 2 * SPAN), BF16),
            pltpu.SMEM((2, 4), jnp.int32),
            pltpu.SMEM((1, 2, 4, 4), jnp.int32),
            pltpu.VMEM((1, MODES), BF16),
            pltpu.VMEM((4 * SPAN, MODES), BF16),
            pltpu.VMEM((2, SPAN, MODES), BF16),
            pltpu.VMEM((2 * SPAN, MODES), BF16),
            pltpu.VMEM((2 * SPAN, MODES), BF16),
            pltpu.VMEM((PART, MODES), BF16),
            pltpu.VMEM((PART, MODES), BF16),
            pltpu.VMEM((8, MODES), F32),
            pltpu.VMEM((8, MODES), F32),
            pltpu.VMEM((8, MODES), F32),
            pltpu.VMEM((3, 32, 2, 8, MODES), F32),
            pltpu.VMEM((3, 32, 8, MODES), F32),
            pltpu.VMEM((3, 3, 64, MODES), BF16),
            pltpu.VMEM((3, 3, 64, MODES), BF16),
            pltpu.VMEM((3, 8, 8, MODES), F32),
            pltpu.VMEM((3, 8, 16, 256), BF16),
            pltpu.VMEM((3, 7, 16, 256), BF16),
            pltpu.VMEM((8, MODES), F32),
            pltpu.VMEM((8, MODES), F32),
            dma((5,)),
            dma((2,)), dma((2,)),
            dma((4, 4)), dma((4, 4)),
            dma((4, 4)), dma((4, 4)),
            dma((2, 4)), dma((2, 4)),
            dma((2,)),
            dma((3,)), dma((3,)),
            dma((3, 3)), dma((3, 3)),
            dma((3, 7)), dma((3, 7)),
            dma((2,)),
            pltpu.SemaphoreType.REGULAR,
        ],
        compiler_params=pltpu.CompilerParams(
            collective_id=0, has_side_effects=True, vmem_limit_bytes=62 << 20
        ),
        cost_estimate=pl.CostEstimate(
            flops=3_000_000_000, bytes_accessed=4_000_000, transcendentals=0
        ),
    )(eigvec, flux, blocks.T, tile_mask, freq)
    return pl.pallas_call(
        hand_out,
        out_shape=tuple(jax.ShapeDtypeStruct(v.shape, v.dtype) for v in sums),
        in_specs=[vmem] * 3,
        out_specs=(vmem, vmem, vmem),
    )(*sums)


def solution(mesh):
    return jax.shard_map(
        shards,
        mesh=mesh,
        in_specs=(
            P("domain", "panel"),
            P("domain", None),
            P("domain", None),
            P("panel", None, None, None),
            P("panel", None),
        ),
        out_specs=(P("panel", "domain", None), P("panel", "domain", None), P("panel", "domain")),
        check_vma=False,
    )
```
